512 devices in a mesh: band: 8 (over z_lo, core), row: 64 (over z_hi, x, y).
Axes of the slice: x: 4, y: 8, z: 8 (z_hi: 2, z_lo: 4; z = z_hi * 4 + z_lo), core: 2. Of those that a mesh axis runs over, the one named last changes fastest.
Arguments:
- latent: float32 [65536, 128], P(('band', 'row')), may hold values from -48 to 48
- input_proj: bfloat16 [2, 128, 1024], P(None, 'row'), may hold values from -0.5 to 0.5
- qkv_proj: bfloat16 [2, 1024, 1536], P(None, 'row'), may hold values from -4 to 4
- mix_proj: bfloat16 [2, 512, 1024], P(None, 'row'), may hold values from -0.25 to 0.25
- affine_head: bfloat16 [2, 1024, 256], P(None, 'row'), may hold values from -0.09375 to 0.09375
- attn_gain: float32 [2, 1024], replicated, may hold values from 0.5 to 1.5
- head_gain: float32 [2, 1024], replicated, may hold values from 0.5 to 1.5
Outputs:
- flow_out: float32 [65536, 128], P(('band', 'row'))
The draws below stay inside these ranges and needn't reach their ends.
All inputs are finite; a program needn't handle non-finite values.
Results may differ from the reference program's by a relative error of at most 0.008.
Values may be sent and summed in bfloat16 or wider, within the bound.
A program may use at most 64 MiB of HBM per device.

```python
import math
import jax
import jax.numpy as jnp
from jax import lax

G = 256
C = 128
D = 1024
HEADS = 4
HS = 128
WIN = 1024
BLOCKS = 2


def draw_latent(key, part):
    key = jax.random.fold_in(key, 11)
    key_base, key_rows, key_cols = jax.random.split(key, 3)
    total_rows = G * G
    row_scale = jnp.exp(jax.random.uniform(key_rows, (total_rows, 1), jnp.float32, math.log(0.3), math.log(3.0)))
    col_scale = jnp.exp(jax.random.uniform(key_cols, (1, C), jnp.float32, math.log(0.4), math.log(4.0)))
    values = jnp.clip(jax.random.normal(key_base, (total_rows, C), jnp.float32), -4.0, 4.0)
    return values * row_scale * col_scale


def draw_qkv_proj(key, part):
    key = jax.random.fold_in(key, 23)
    key_query, key_key, key_value = jax.random.split(key, 3)
    full_shape = (BLOCKS, D, HEADS * HS)
    query_part = jnp.clip(jax.random.normal(key_query, full_shape, jnp.float32), -4.0, 4.0) / math.sqrt(D)
    key_part = jnp.clip(jax.random.normal(key_key, full_shape, jnp.float32), -4.0, 4.0) / math.sqrt(D)
    value_part = jnp.clip(jax.random.normal(key_value, full_shape, jnp.float32), -4.0, 4.0) / math.sqrt(D)
    return jnp.concatenate([query_part, key_part, value_part], axis=2).astype(jnp.bfloat16)


def shard_levels(stream_key, extent, shards, smallest, high):
    loudness, own = 1.0, jax.random.fold_in(stream_key, 6)
    for dim, shards_of in shards:
        steps = jnp.exp(jax.random.uniform(jax.random.fold_in(own, dim), (shards_of,), jnp.float32, smallest / len(shards), high / len(shards)))
        loudness = loudness * jnp.repeat(steps, extent[dim] // shards_of).reshape([-1 if axis == dim else 1 for axis in range(len(extent))])
    return loudness


def scatter_about(key, extent, deviation, limit, cuts=(), kind=jnp.bfloat16):
    values = deviation * jax.random.normal(key, extent, jnp.float32)
    if cuts:
        values = values * shard_levels(key, extent, cuts, -0.22, 0.18)
    return jnp.clip(values, -limit, limit).astype(kind)


def setup_inputs(seed: int = 0) -> dict:
    streams_of = jax.random.split(jax.random.key(seed), 8)
    return {
        "latent": draw_latent(jax.random.fold_in(streams_of[7], 71), 0),
        "input_proj": scatter_about(streams_of[1], (BLOCKS, C, D), C ** -0.5, 0.5, ((1, 64),)),
        "qkv_proj": draw_qkv_proj(jax.random.fold_in(streams_of[7], 71), 0),
        "mix_proj": scatter_about(streams_of[3], (BLOCKS, HEADS * HS, D), (HEADS * HS) ** -0.5, 0.25, ((1, 64),)),
        "affine_head": scatter_about(streams_of[4], (BLOCKS, D, 2 * C), (4 * D) ** -0.5, 0.09375, ((1, 64),)),
        "attn_gain": jnp.clip(1.0 + 0.1 * jax.random.normal(streams_of[5], (BLOCKS, D), jnp.float32), 0.5, 1.5),
        "head_gain": jnp.clip(1.0 + 0.1 * jax.random.normal(streams_of[6], (BLOCKS, D), jnp.float32), 0.5, 1.5),
    }


EPS = 1e-06

def normed(values, gains):
    inverse = lax.rsqrt(lax.optimization_barrier(jnp.mean(values * values, axis=-1, keepdims=True)) + EPS)
    return (values * inverse * gains).astype(jnp.bfloat16)

def attend(query_rows, window_keys, query_pos, key_pos):
    inner_width = HEADS * HS
    queries = query_rows.astype(jnp.float32).reshape(-1, HEADS, HS)
    key_part = window_keys[:, :inner_width].astype(jnp.float32).reshape(-1, HEADS, HS)
    value_part = window_keys[:, inner_width:].astype(jnp.float32).reshape(-1, HEADS, HS)
    scores = jnp.einsum('qhd,khd->hqk', queries, key_part) * (1.0 / math.sqrt(HS))
    allowed = (key_pos[None, :] <= query_pos[:, None]) & (key_pos[None, :] > query_pos[:, None] - WIN) & (key_pos[None, :] >= 0)
    scores = jnp.where(allowed[None], scores, -1e+30)
    highest = lax.optimization_barrier(jnp.max(scores, axis=-1, keepdims=True))
    weights = jnp.exp(scores - highest)
    probs = (weights / lax.optimization_barrier(jnp.sum(weights, axis=-1, keepdims=True))).astype(jnp.bfloat16)
    result = jnp.einsum('hqk,khd->qhd', probs.astype(jnp.float32), value_part)
    return result.reshape(-1, inner_width).astype(jnp.bfloat16)

def window_attention(projected):
    total_rows = projected.shape[0]
    inner_width = HEADS * HS
    block_rows = min(total_rows, 512)
    block_count = total_rows // block_rows
    padded = jnp.concatenate([jnp.zeros((WIN, 2 * inner_width), jnp.bfloat16), projected[:, inner_width:]], axis=0)
    grouped = projected[:, :inner_width].reshape(block_count, block_rows, inner_width)

    def one_block(packed):
        query_rows, block_index = packed
        offset = block_index * block_rows
        window_keys = lax.dynamic_slice_in_dim(padded, offset, WIN + block_rows, 0)
        query_pos = offset + jnp.arange(block_rows, dtype=jnp.int32)
        key_pos = offset - WIN + jnp.arange(WIN + block_rows, dtype=jnp.int32)
        return attend(query_rows, window_keys, query_pos, key_pos)
    result = lax.map(one_block, (grouped, jnp.arange(block_count, dtype=jnp.int32)))
    return result.reshape(total_rows, inner_width)

def flow_block(flow_state, w_in, w_qkv, w_mix, w_head, gain_attn, gain_head):
    rounded = flow_state.astype(jnp.bfloat16)
    hidden = jnp.dot(rounded, w_in, preferred_element_type=jnp.float32)
    projected = jnp.dot(normed(hidden, gain_attn), w_qkv, preferred_element_type=jnp.float32).astype(jnp.bfloat16)
    attended = window_attention(projected)
    hidden = hidden + jnp.dot(attended, w_mix, preferred_element_type=jnp.float32)
    params = jnp.dot(normed(hidden, gain_head), w_head, preferred_element_type=jnp.float32)
    shifted = jnp.concatenate([jnp.zeros((1, 2 * C), jnp.float32), params[:-1]], axis=0)
    return (flow_state - shifted[:, :C]) * jnp.exp(-shifted[:, C:])

def reference(latent, input_proj, qkv_proj, mix_proj, affine_head, attn_gain, head_gain):
    flow_state = latent
    for section_index in range(BLOCKS):
        if section_index > 0:
            flow_state = flow_state.reshape(G, G, C).transpose(1, 0, 2).reshape(G * G, C)
        flow_state = flow_block(flow_state, input_proj[section_index], qkv_proj[section_index], mix_proj[section_index], affine_head[section_index], attn_gain[section_index], head_gain[section_index])
    return flow_state
```

```python
import math

import jax
import jax.numpy as jnp
from jax import lax
from jax.experimental import pallas as pl
from jax.experimental.pallas import tpu as pltpu
from jax.sharding import PartitionSpec as P

MESH = pl.DeviceIdType.MESH
F32, BF16 = jnp.float32, jnp.bfloat16
G, C, D, HEADS, HS, WIN = 256, 128, 1024, 4, 128, 1024
INNER = HEADS * HS
TOK = 128
DEVICES = 512
NA = INNER + INNER + 256
NB = 128 + 2 * INNER
EXTRA = 16
ROWS = EXTRA + TOK
T0 = WIN + TOK
T1 = 5 * G
EPS = 1e-06
SCALE = math.log2(math.e) / math.sqrt(HS)


def place():
    band, row = lax.axis_index("band"), lax.axis_index("row")
    return band, row, band // 2, band % 2, row // 32, (row // 8) % 4, row % 8


def at_device(index):
    return (index // 64, index % 64)


class Gather:
    def __init__(self, wa, wb, sems):
        self.wa, self.wb, self.s = wa, wb, sems
        self.band, self.row, self.zlo, self.core, self.zhi, self.x, self.y = place()
        self.sent = ({}, {})

    def at(self, x=None, y=None, zhi=None, core=None):
        x = self.x if x is None else x
        y = self.y if y is None else y
        zhi = self.zhi if zhi is None else zhi
        core = self.core if core is None else core
        return (self.zlo * 2 + core, zhi * 32 + x * 8 + y)

    def copy(self, ref, sem, where):
        name, *index = sem
        return pltpu.make_async_remote_copy(
            src_ref=ref,
            dst_ref=ref,
            send_sem=self.s[name][0].at[*index],
            recv_sem=self.s[name][1].at[*index],
            device_id=where,
            device_id_type=MESH,
        )

    def send(self, core, ref, sem, where):
        self.copy(ref, sem, where).start()
        kind = "half" if sem[0] == "side" else "column" if len(ref.shape) == 3 else "cell" if ref.shape[0] == 16 else "line"
        self.sent[core][sem] = kind

    def got(self, ref, sem):
        self.copy(ref, sem, self.at()).wait_recv()

    def half(self, h):
        return self.zhi if h == 0 else 1 - self.zhi

    def cell(self, w, b, h, x, y):
        return w.at[b, 4 * self.half(h) + x, pl.ds(pl.multiple_of(16 * y, 16), 16)]

    def column(self, w, b, h, y):
        return w.at[b, pl.ds(4 * self.half(h), 4), pl.ds(pl.multiple_of(16 * y, 16), 16)]

    def line(self, w, b, h, x):
        return w.at[b, 4 * self.half(h) + x]

    def across(self, core, b):
        w = (self.wa, self.wb)[core]
        self.send(core, self.cell(w, b, 0, self.x, self.y), ("z", b), self.at(zhi=1 - self.zhi))

    def across_got(self, core, b):
        w = (self.wa, self.wb)[core]
        self.got(self.cell(w, b, 1, self.x, self.y), ("z", b))

    def a_x(self, b, h):
        for d in (1, 3, 2):
            self.send(0, self.cell(self.wa, b, h, self.x, self.y), ("ax", b, h, d), self.at(x=(self.x + d) % 4))

    def a_side(self, b, h, y):
        self.send(0, self.column(self.wa, b, h, y), ("side", b, h), self.at(core=1))

    def a_y(self, b, h, k):
        last = (4, 3) if h == 0 else (3, 4)
        if k == 0:
            for d in (1, 3, 2):
                self.got(self.cell(self.wa, b, h, (self.x - d) % 4, self.y), ("ax", b, h, d))
        for way, step in ((0, 1), (1, -1)):
            if k > last[way]:
                continue
            y = (self.y - step * k) % 8
            ref = self.column(self.wa, b, h, y)
            if k > 0:
                self.got(ref, ("ay", b, h, way, k))
            if k < last[way]:
                self.send(0, ref, ("ay", b, h, way, k + 1), self.at(y=(self.y + step) % 8))
            if k > 0 or way == 0:
                self.a_side(b, h, y)

    def b_y(self, b, h):
        for d in (4, 3, 5, 2, 6, 1, 7):
            self.send(1, self.cell(self.wb, b, h, self.x, self.y), ("by", b, h, d), self.at(y=(self.y + d) % 8))

    def b_x(self, b, h):
        for d in range(1, 8):
            self.got(self.cell(self.wb, b, h, self.x, (self.y - d) % 8), ("by", b, h, d))
        for d in (2, 1, 3):
            self.send(1, self.line(self.wb, b, h, self.x), ("bx", b, h, d), self.at(x=(self.x + d) % 4))
        self.b_side(b, h, self.x)

    def b_side(self, b, h, x):
        self.send(1, self.line(self.wb, b, h, x), ("side", b, h), self.at(core=0))

    def b_on(self, b, h, d):
        x = (self.x - d) % 4
        self.got(self.line(self.wb, b, h, x), ("bx", b, h, d))
        self.b_side(b, h, x)

    def side_got(self, core, b):
        w = (self.wb, self.wa)[core]
        for h in range(2):
            self.got(w.at[b, pl.ds(4 * self.half(h), 4)], ("side", b, h))

    def steps(self, core, b):
        if core == 0:
            yield lambda: self.across(0, b)
            yield lambda: self.a_x(b, 0)
            yield lambda: (self.across_got(0, b), self.a_x(b, 1))
            for k in range(5):
                yield lambda k=k: (self.a_y(b, 0, k), self.a_y(b, 1, k))
        else:
            yield lambda: self.across(1, b)
            yield lambda: self.b_y(b, 0)
            yield lambda: (self.across_got(1, b), self.b_y(b, 1))
            yield lambda: self.b_x(b, 0)
            yield lambda: self.b_x(b, 1)
            yield lambda: (self.b_on(b, 0, 1), self.b_on(b, 0, 3), self.b_on(b, 0, 2))
            yield lambda: (self.b_on(b, 1, 1), self.b_on(b, 1, 3), self.b_on(b, 1, 2))
            yield lambda: None
        yield lambda: self.side_got(core, b)

    def run(self, pairs):
        for first, second in pairs:
            pl.when(self.core == 0)(lambda: (first(), None)[1])
            pl.when(self.core == 1)(lambda: (second(), None)[1])

    def finish(self):
        for core in range(2):

            @pl.when(self.core == core)
            def _():
                w = (self.wa, self.wb)[core]
                whole = dict(
                    cell=w.at[0, 0, pl.ds(0, 16)],
                    column=w.at[0, pl.ds(0, 4), pl.ds(0, 16)],
                    line=w.at[0, 0],
                    half=w.at[0, pl.ds(0, 4)],
                )
                for sem, kind in self.sent[core].items():
                    self.copy(whole[kind], sem, self.at()).wait_send()


def inverse_rms(values):
    return lax.rsqrt(jnp.mean(values * values, axis=-1, keepdims=True) + EPS)


def kernel(
    latent, w_in, w_qkv, w_mix, w_head, gain_attn, gain_head, out,
    wa, wb, win, wmix, unpack, halo, tile_a, tile_b, grid_rows, natural, query_state,
    normed, pairs, attended, params, state,
    zsem, zsend, axsem, axsend, aysem, aysend, bysem, bysend, bxsem, bxsend, side, side_send,
    hsend, hrecv, dsend, drecv, esend, erecv, local_sem,
):
    band, row, zlo, core, zhi, x, y = place()
    me = band * 64 + row
    before, after = jnp.minimum(me, 8), jnp.minimum(DEVICES - 1 - me, 8)

    barrier = pltpu.get_barrier_semaphore()

    def greet(where):
        pl.semaphore_signal(barrier, inc=1, device_id=where, device_id_type=MESH)

    for d in range(1, 8):
        greet((band, row - y + (y + d) % 8))
    for d in range(1, 4):
        greet((band, zhi * 32 + ((x + d) % 4) * 8 + y))
    for d in range(1, 16):
        other = (band * 2 + zhi + d) % 16
        greet((other // 2, (other % 2) * 32 + x * 8 + y))
    for d in range(1, 9):
        pl.when(me >= d)(lambda d=d: greet(at_device(me - d)))
        pl.when(me + d < DEVICES)(lambda d=d: greet(at_device(me + d)))

    mine = pl.ds(pl.multiple_of(16 * y, 16), 16)

    @pl.when(core == 0)
    def _():
        for b in range(2):
            wa[b, 4 * zhi + x, mine, 0:INNER] = w_qkv[b, :, 0:INNER]
            mix = w_mix[b].astype(F32)
            wa[b, 4 * zhi + x, mine, INNER : 2 * INNER] = jnp.concatenate(
                [mix[:, :512], mix[:, 512:]], axis=0
            ).astype(BF16)
            wa[b, 4 * zhi + x, mine, 2 * INNER :] = w_head[b]

    @pl.when(core == 1)
    def _():
        for b in range(2):
            wide = w_in[b].astype(F32)
            wb[b, 4 * zhi + x, mine, 0:128] = jnp.concatenate(
                [wide[a : a + 1, 128 * g : 128 * g + 128] for a in range(2) for g in range(8)], axis=0
            ).astype(BF16)
            wb[b, 4 * zhi + x, mine, 128:] = w_qkv[b, :, INNER:]

    halo[8 * TOK :, :] = latent[...].astype(BF16)

    def clear(k, _):
        halo[pl.ds(pl.multiple_of(k * TOK, TOK), TOK), :] = jnp.zeros((TOK, C), BF16)
        return 0

    lax.fori_loop(0, 8 - before, clear, 0)
    column = me // 2
    lower = me % 2

    def clear_column(k, _):
        grid_rows[k] = jnp.zeros((16, 16, C), BF16)
        return 0

    lax.fori_loop(0, jnp.maximum(4 - column, 0), clear_column, 0)

    pl.semaphore_wait(barrier, 25 + before + after)

    sems = dict(
        z=(zsend, zsem),
        ax=(axsend, axsem),
        ay=(aysend, aysem),
        by=(bysend, bysem),
        bx=(bxsend, bxsem),
        side=(side_send, side),
    )
    gather = Gather(wa, wb, sems)
    steps = [list(zip(gather.steps(0, b), gather.steps(1, b))) for b in range(2)]

    def halo_copy(d):
        return pltpu.make_async_remote_copy(
            src_ref=halo.at[pl.ds(8 * TOK, TOK)],
            dst_ref=halo.at[pl.ds((8 - d) * TOK, TOK)],
            send_sem=hsend.at[d],
            recv_sem=hrecv.at[d],
            device_id=at_device(me + d),
            device_id_type=MESH,
        )

    gather.run(steps[0][:2])
    for d in range(1, 9):
        pl.when(me + d < DEVICES)(lambda d=d: halo_copy(d).start())
    gather.run(steps[0][2:])
    gather.run(steps[1])

    for d in range(1, 9):
        pl.when(me >= d)(lambda d=d: halo_copy(d).wait_recv())

    def block(b, window, tokens, chunk, query_rows, key_pos, first_query, first_pos):
        unpack[...] = wb[b, :, :, 0:128].reshape(D, 128).astype(F32)
        for g in range(8):
            win[:, 128 * g : 128 * g + 128] = unpack[pl.ds(g, 128, stride=8), :].astype(BF16)
        packed = wa[b, :, :, INNER : 2 * INNER].reshape(64, 16, 512).astype(F32)
        for part in range(2):
            wmix[:, 512 * part : 512 * part + 512] = packed[:, 8 * part : 8 * part + 8].reshape(512, 512).astype(BF16)

        gain = gain_attn[b : b + 1, :]

        def keys(k, _):
            rows = pl.ds(pl.multiple_of(k * chunk, chunk), chunk)
            hidden = jnp.dot(window(k, chunk), win[...], preferred_element_type=F32)
            normed[0:chunk, :] = (hidden * inverse_rms(hidden) * gain).astype(BF16)
            for part in range(2):
                weights = wb[b, :, :, 128 + 512 * part : 640 + 512 * part].reshape(D, 512)
                pairs[rows, 512 * part : 512 * part + 512] = jnp.dot(
                    normed[0:chunk, :], weights, preferred_element_type=F32
                ).astype(BF16)
            return 0

        lax.fori_loop(0, tokens // chunk, keys, 0)
        hidden = jnp.dot(query_rows, win[...], preferred_element_type=F32)
        queries = jnp.dot(
            (hidden * inverse_rms(hidden) * gain).astype(BF16),
            wa[b, :, :, 0:INNER].reshape(D, INNER),
            preferred_element_type=F32,
        ).astype(BF16)
        query_pos = lax.broadcasted_iota(jnp.int32, (ROWS, 1), 0) + first_query
        allowed = (key_pos <= query_pos) & (key_pos > query_pos - WIN) & (key_pos + first_pos >= 0)
        for head in range(HEADS):
            lanes = slice(HS * head, HS * head + HS)
            scores = lax.dot_general(
                queries[:, lanes], pairs[0:tokens, lanes], (((1,), (1,)), ((), ())), preferred_element_type=F32
            )
            scores = jnp.where(allowed, scores, -1e30)
            weights = jnp.exp2((scores - jnp.max(scores, axis=-1, keepdims=True)) * SCALE)
            total = jnp.sum(weights, axis=-1, keepdims=True)
            values = pairs[0:tokens, INNER + HS * head : INNER + HS * head + HS]
            result = jnp.dot(weights.astype(BF16), values, preferred_element_type=F32)
            attended[:, lanes] = (result / total).astype(BF16)
        hidden = hidden + jnp.dot(attended[...], wmix[...], preferred_element_type=F32)
        params[...] = jnp.dot(
            (hidden * inverse_rms(hidden) * gain_head[b : b + 1, :]).astype(BF16),
            wa[b, :, :, 2 * INNER :].reshape(D, 256),
            preferred_element_type=F32,
        )
        shifted = params[EXTRA - 1 : EXTRA - 1 + TOK, :]
        first = (lax.broadcasted_iota(jnp.int32, (TOK, 1), 0) == 0) & (me == 0)
        return jnp.where(first, 0.0, shifted)

    position = lax.broadcasted_iota(jnp.int32, (1, T0), 1)
    shifted = block(
        0,
        lambda k, n: halo[pl.ds(pl.multiple_of(k * n, n), n), :],
        T0,
        384,
        halo[WIN - EXTRA :, :],
        position,
        WIN - EXTRA,
        me * TOK - WIN,
    )
    state[...] = ((latent[...] - shifted[:, :C]) * jnp.exp(-shifted[:, C:])).astype(BF16)

    source = band * 2 + zhi
    high = y % 2

    def first_stage(g):
        return (high * 2 + g // 4) * 4 + g % 4

    def stage_copy(g):
        target = first_stage(g)
        return pltpu.make_async_remote_copy(
            src_ref=state.at[pl.ds(pl.multiple_of(16 * g, 16), 16)],
            dst_ref=tile_a.at[source],
            send_sem=dsend.at[g],
            recv_sem=drecv,
            device_id=(target // 2, (target % 2) * 32 + x * 8 + y),
            device_id_type=MESH,
        )

    def stage_local(g):
        return pltpu.make_async_copy(
            state.at[pl.ds(pl.multiple_of(16 * g, 16), 16)], tile_a.at[source], local_sem
        )

    for g in range(8):
        mine_too = first_stage(g) == source
        pl.when(mine_too)(lambda g=g: stage_local(g).start())
        pl.when(jnp.logical_not(mine_too))(lambda g=g: stage_copy(g).start())

    relay = zlo // 2 == high
    base = 16 * source
    residue = x * 4 + y // 2
    own_offset = x * 4 + y // 2

    def second_copy(o, half, n, at, slot):
        return pltpu.make_async_remote_copy(
            src_ref=tile_b.at[pl.ds(at, n)],
            dst_ref=grid_rows.at[pl.ds(slot, n), residue],
            send_sem=esend.at[2 * o + half],
            recv_sem=erecv,
            device_id=at_device(2 * (base + o) + half),
            device_id_type=MESH,
        )

    def second_local(o, n, at, slot):
        return pltpu.make_async_copy(tile_b.at[pl.ds(at, n)], grid_rows.at[pl.ds(slot, n), residue], erecv)

    def second_each(act, act_local):
        for o in range(20):
            at, slot = max(o - 4, 0), max(4 - o, 0)
            n = min(o, 15) - at + 1
            for half in range(2):
                if o < 16:
                    ours = (own_offset == o) & (y % 2 == half)
                    if act_local is not None:
                        pl.when(ours)(lambda: act_local(second_local(o, n, at, slot)))
                    pl.when(jnp.logical_not(ours))(lambda: act(second_copy(o, half, n, at, slot)))
                else:
                    pl.when(base + o < G)(lambda: act(second_copy(o, half, n, at, slot)))

    @pl.when(relay)
    def _():
        for g in range(8):
            pl.when(first_stage(g) == source)(lambda g=g: stage_local(g).wait())

        pltpu.make_async_remote_copy(
            src_ref=tile_a.at[pl.ds(0, 15)],
            dst_ref=tile_a.at[pl.ds(0, 15)],
            send_sem=dsend.at[0],
            recv_sem=drecv,
            device_id=(band, row),
            device_id_type=MESH,
        ).wait_recv()
        unpack[0:256, :] = tile_a[...].reshape(256, C).astype(F32)
        for c in range(16):
            tile_b[c] = unpack[pl.ds(c, 16, stride=16), :].astype(BF16)
        second_each(lambda copy: copy.start(), lambda copy: copy.start())

    def slots_got(n):
        pltpu.make_async_remote_copy(
            src_ref=grid_rows.at[pl.ds(5 - n, n)],
            dst_ref=grid_rows.at[pl.ds(5 - n, n)],
            send_sem=esend.at[0],
            recv_sem=erecv,
            device_id=(band, row),
            device_id_type=MESH,
        ).wait_recv()

    for n in range(1, 6):
        pl.when(column + 1 == n if n < 5 else column >= 4)(lambda n=n: slots_got(n))

    unpack[0:256, :] = grid_rows[3].reshape(256, C).astype(F32)
    natural[0:16, :] = unpack[pl.ds(15, 16, stride=16), :]
    unpack[0:256, :] = grid_rows[4].reshape(256, C).astype(F32)
    for m in range(16):
        natural[16 + 16 * m : 32 + 16 * m, :] = unpack[pl.ds(m, 16, stride=16), :]
    query_state[...] = natural[pl.ds(pl.multiple_of(lower * TOK, TOK), ROWS), :]

    place_in = lax.broadcasted_iota(jnp.int32, (1, T1), 1)
    position = place_in // 256 * 256 + place_in % 16 * 16 + place_in // 16 % 16
    shifted = block(
        1,
        lambda k, n: grid_rows[k].reshape(256, C),
        T1,
        256,
        query_state[...].astype(BF16),
        position,
        WIN - EXTRA + lower * TOK,
        (column - 4) * G,
    )
    out[...] = (query_state[EXTRA:, :] - shifted[:, :C]) * jnp.exp(-shifted[:, C:])

    gather.finish()
    for d in range(1, 9):
        pl.when(me + d < DEVICES)(lambda d=d: halo_copy(d).wait_send())
    for g in range(8):
        pl.when(first_stage(g) != source)(lambda g=g: stage_copy(g).wait_send())

    @pl.when(relay)
    def _():
        second_each(lambda copy: copy.wait_send(), None)


def shards(*args):
    vmem = pl.BlockSpec(memory_space=pltpu.VMEM)
    dma = pltpu.SemaphoreType.DMA
    return pl.pallas_call(
        kernel,
        out_shape=jax.ShapeDtypeStruct((TOK, C), F32),
        in_specs=[vmem] * 7,
        out_specs=vmem,
        scratch_shapes=[
            pltpu.VMEM((2, 8, 128, NA), BF16),
            pltpu.VMEM((2, 8, 128, NB), BF16),
            pltpu.VMEM((C, D), BF16),
            pltpu.VMEM((INNER, D), BF16),
            pltpu.VMEM((D, 128), F32),
            pltpu.VMEM((9 * TOK, C), BF16),
            pltpu.VMEM((16, 16, C), BF16),
            pltpu.VMEM((16, 16, C), BF16),
            pltpu.VMEM((5, 16, 16, C), BF16),
            pltpu.VMEM((17 * 16, C), F32),
            pltpu.VMEM((ROWS, C), F32),
            pltpu.VMEM((384, D), BF16),
            pltpu.VMEM((T1, 2 * INNER), BF16),
            pltpu.VMEM((ROWS, INNER), BF16),
            pltpu.VMEM((ROWS, 256), F32),
            pltpu.VMEM((TOK, C), BF16),
            *[dma(shape) for shape in ((2,), (2, 2, 4), (2, 2, 2, 5), (2, 2, 8), (2, 2, 4), (2, 2)) for _ in range(2)],
            dma((9,)),
            dma((9,)),
            dma((8,)),
            dma(()),
            dma((40,)),
            dma(()),
            dma(()),
        ],
        compiler_params=pltpu.CompilerParams(collective_id=0, has_side_effects=True, vmem_limit_bytes=56 << 20),
    )(*args)


def solution(mesh):
    return jax.shard_map(
        shards,
        mesh=mesh,
        in_specs=(
            P(("band", "row"), None),
            P(None, "row", None),
            P(None, "row", None),
            P(None, "row", None),
            P(None, "row", None),
            P(),
            P(),
        ),
        out_specs=P(("band", "row"), None),
        check_vma=False,
    )
```

```python
import math

import jax
import jax.numpy as jnp
from jax import lax
from jax.experimental import pallas as pl
from jax.experimental.pallas import tpu as pltpu
from jax.sharding import PartitionSpec as P

MESH = pl.DeviceIdType.MESH
F32, BF16 = jnp.float32, jnp.bfloat16
G, C, D, HEADS, HS, WIN = 256, 128, 1024, 4, 128, 1024
INNER = HEADS * HS
TOK = 128
DEVICES = 512
NA = INNER + INNER + 256
NB = 128 + 2 * INNER
EXTRA = 16
ROWS = EXTRA + TOK
T0 = WIN + TOK
T1 = 5 * G
EPS = 1e-06
HOOKS = (2, 3, 3, 4, 4, 5, 6)
SCALE = math.log2(math.e) / math.sqrt(HS)


def place():
    band, row = lax.axis_index("band"), lax.axis_index("row")
    return band, row, band // 2, band % 2, row // 32, (row // 8) % 4, row % 8


def at_device(index):
    return (index // 64, index % 64)


class Gather:
    def __init__(self, wa, wb, sems):
        self.wa, self.wb, self.s = wa, wb, sems
        self.band, self.row, self.zlo, self.core, self.zhi, self.x, self.y = place()
        self.sent = ({}, {})

    def at(self, x=None, y=None, zhi=None, core=None):
        x = self.x if x is None else x
        y = self.y if y is None else y
        zhi = self.zhi if zhi is None else zhi
        core = self.core if core is None else core
        return (self.zlo * 2 + core, zhi * 32 + x * 8 + y)

    def copy(self, ref, sem, where):
        name, *index = sem
        return pltpu.make_async_remote_copy(
            src_ref=ref,
            dst_ref=ref,
            send_sem=self.s[name][0].at[*index],
            recv_sem=self.s[name][1].at[*index],
            device_id=where,
            device_id_type=MESH,
        )

    def send(self, core, ref, sem, where):
        self.copy(ref, sem, where).start()
        kind = "half" if sem[0] == "side" else "column" if len(ref.shape) == 3 else "cell" if ref.shape[0] == 16 else "line"
        self.sent[core][sem] = kind

    def got(self, ref, sem):
        self.copy(ref, sem, self.at()).wait_recv()

    def half(self, h):
        return self.zhi if h == 0 else 1 - self.zhi

    def cell(self, w, b, h, x, y):
        return w.at[b, 4 * self.half(h) + x, pl.ds(pl.multiple_of(16 * y, 16), 16)]

    def column(self, w, b, h, y):
        return w.at[b, pl.ds(4 * self.half(h), 4), pl.ds(pl.multiple_of(16 * y, 16), 16)]

    def line(self, w, b, h, x):
        return w.at[b, 4 * self.half(h) + x]

    def across(self, core, b):
        w = (self.wa, self.wb)[core]
        self.send(core, self.cell(w, b, 0, self.x, self.y), ("z", b), self.at(zhi=1 - self.zhi))

    def across_got(self, core, b):
        w = (self.wa, self.wb)[core]
        self.got(self.cell(w, b, 1, self.x, self.y), ("z", b))

    def a_x(self, b, h):
        for d in (1, 3, 2):
            self.send(0, self.cell(self.wa, b, h, self.x, self.y), ("ax", b, h, d), self.at(x=(self.x + d) % 4))

    def a_side(self, b, h, y):
        self.send(0, self.column(self.wa, b, h, y), ("side", b, h), self.at(core=1))

    def a_y(self, b, h, k):
        last = (4, 3) if h == 0 else (3, 4)
        if k == 0:
            for d in (1, 3, 2):
                self.got(self.cell(self.wa, b, h, (self.x - d) % 4, self.y), ("ax", b, h, d))
        for way, step in ((0, 1), (1, -1)):
            if k > last[way]:
                continue
            y = (self.y - step * k) % 8
            ref = self.column(self.wa, b, h, y)
            if k > 0:
                self.got(ref, ("ay", b, h, way, k))
            if k < last[way]:
                self.send(0, ref, ("ay", b, h, way, k + 1), self.at(y=(self.y + step) % 8))
            if k > 0 or way == 0:
                self.a_side(b, h, y)

    def b_y(self, b, h):
        for d in (4, 3, 5, 2, 6, 1, 7):
            self.send(1, self.cell(self.wb, b, h, self.x, self.y), ("by", b, h, d), self.at(y=(self.y + d) % 8))

    def b_x(self, b, h):
        for d in range(1, 8):
            self.got(self.cell(self.wb, b, h, self.x, (self.y - d) % 8), ("by", b, h, d))
        for d in (2, 1, 3):
            self.send(1, self.line(self.wb, b, h, self.x), ("bx", b, h, d), self.at(x=(self.x + d) % 4))
        self.b_side(b, h, self.x)

    def b_side(self, b, h, x):
        self.send(1, self.line(self.wb, b, h, x), ("side", b, h), self.at(core=0))

    def b_on(self, b, h, d):
        x = (self.x - d) % 4
        self.got(self.line(self.wb, b, h, x), ("bx", b, h, d))
        self.b_side(b, h, x)

    def side_got(self, core, b):
        w = (self.wb, self.wa)[core]
        for h in range(2):
            self.got(w.at[b, pl.ds(4 * self.half(h), 4)], ("side", b, h))

    def steps(self, core, b):
        if core == 0:
            yield lambda: self.across(0, b)
            yield lambda: self.a_x(b, 0)
            yield lambda: (self.across_got(0, b), self.a_x(b, 1))
            for k in range(5):
                yield lambda k=k: (self.a_y(b, 0, k), self.a_y(b, 1, k))
        else:
            yield lambda: self.across(1, b)
            yield lambda: self.b_y(b, 0)
            yield lambda: (self.across_got(1, b), self.b_y(b, 1))
            yield lambda: self.b_x(b, 0)
            yield lambda: self.b_x(b, 1)
            yield lambda: (self.b_on(b, 0, 1), self.b_on(b, 0, 3), self.b_on(b, 0, 2))
            yield lambda: (self.b_on(b, 1, 1), self.b_on(b, 1, 3), self.b_on(b, 1, 2))
            yield lambda: None
        yield lambda: self.side_got(core, b)

    def run(self, pairs):
        for first, second in pairs:
            pl.when(self.core == 0)(lambda: (first(), None)[1])
            pl.when(self.core == 1)(lambda: (second(), None)[1])

    def finish(self):
        for core in range(2):

            @pl.when(self.core == core)
            def _():
                w = (self.wa, self.wb)[core]
                whole = dict(
                    cell=w.at[0, 0, pl.ds(0, 16)],
                    column=w.at[0, pl.ds(0, 4), pl.ds(0, 16)],
                    line=w.at[0, 0],
                    half=w.at[0, pl.ds(0, 4)],
                )
                for sem, kind in self.sent[core].items():
                    self.copy(whole[kind], sem, self.at()).wait_send()


def inverse_rms(values):
    return lax.rsqrt(jnp.mean(values * values, axis=-1, keepdims=True) + EPS)


def kernel(
    latent, w_in, w_qkv, w_mix, w_head, gain_attn, gain_head, out,
    wa, wb, win, wmix, unpack, halo, tile_a, tile_b, grid_rows, natural, query_state,
    normed, pairs, attended, params, state,
    zsem, zsend, axsem, axsend, aysem, aysend, bysem, bysend, bxsem, bxsend, side, side_send,
    hsend, hrecv, dsend, drecv, esend, erecv, local_sem, ready,
):
    band, row, zlo, core, zhi, x, y = place()
    me = band * 64 + row
    before = jnp.minimum(me, 8)

    barrier = pltpu.get_barrier_semaphore()

    def greet(where):
        pl.semaphore_signal(barrier, inc=1, device_id=where, device_id_type=MESH)

    for d in range(1, 8):
        greet((band, row - y + (y + d) % 8))
    for d in range(1, 4):
        greet((band, zhi * 32 + ((x + d) % 4) * 8 + y))
    for d in range(1, 4):
        greet((((zlo + d) % 4) * 2 + core, row))
    greet((band, (row + 32) % 64))
    greet((zlo * 2 + 1 - core, row))
    tail = row >= 56
    upper, under = tail & (core == 1) & (zlo < 3), tail & (core == 0) & (zlo > 0)
    pl.when(upper)(lambda: greet((band + 1, row)))
    pl.when(under)(lambda: greet((band - 1, row)))

    mine = pl.ds(pl.multiple_of(16 * y, 16), 16)

    @pl.when(core == 0)
    def _():
        for b in range(2):
            wa[b, 4 * zhi + x, mine, 0:INNER] = w_qkv[b, :, 0:INNER]
            mix = w_mix[b].astype(F32)
            wa[b, 4 * zhi + x, mine, INNER : 2 * INNER] = jnp.concatenate(
                [mix[:, :512], mix[:, 512:]], axis=0
            ).astype(BF16)
            wa[b, 4 * zhi + x, mine, 2 * INNER :] = w_head[b]

    @pl.when(core == 1)
    def _():
        for b in range(2):
            wide = w_in[b].astype(F32)
            wb[b, 4 * zhi + x, mine, 0:128] = jnp.concatenate(
                [wide[a : a + 1, 128 * g : 128 * g + 128] for a in range(2) for g in range(8)], axis=0
            ).astype(BF16)
            wb[b, 4 * zhi + x, mine, 128:] = w_qkv[b, :, INNER:]

    halo[8 * TOK :, :] = latent[...].astype(BF16)

    def clear(k, _):
        halo[pl.ds(pl.multiple_of(k * TOK, TOK), TOK), :] = jnp.zeros((TOK, C), BF16)
        return 0

    lax.fori_loop(0, 8 - before, clear, 0)
    column = me // 2
    lower = me % 2

    def clear_column(k, _):
        grid_rows[k] = jnp.zeros((16, 16, C), BF16)
        return 0

    lax.fori_loop(0, jnp.maximum(4 - column, 0), clear_column, 0)

    pl.semaphore_wait(barrier, 15 + (upper | under).astype(jnp.int32))

    sems = dict(
        z=(zsend, zsem),
        ax=(axsend, axsem),
        ay=(aysend, aysem),
        by=(bysend, bysem),
        bx=(bxsend, bxsem),
        side=(side_send, side),
    )
    gather = Gather(wa, wb, sems)
    steps = [list(zip(gather.steps(0, b), gather.steps(1, b))) for b in range(2)]

    def halo_copy(d):
        return pltpu.make_async_remote_copy(
            src_ref=halo.at[pl.ds(8 * TOK, TOK)],
            dst_ref=halo.at[pl.ds((8 - d) * TOK, TOK)],
            send_sem=hsend.at[d],
            recv_sem=hrecv.at[d],
            device_id=at_device(me + d),
            device_id_type=MESH,
        )

    gather.run(steps[0][:5])
    for d in range(1, 9):
        pl.when(row + d < 64)(lambda d=d: halo_copy(d).start())

    @pl.when(tail & (band > 0))
    def _():
        pl.semaphore_signal(ready, inc=1, device_id=(band - 1, row), device_id_type=MESH)

    gather.run(steps[0][5:6])

    @pl.when(tail & (band < 7))
    def _():
        pl.semaphore_wait(ready, 1)
        for d in range(1, 9):
            pl.when(row + d >= 64)(lambda d=d: halo_copy(d).start())

    gather.run(steps[0][6:])
    gather.run(steps[1][:2])
    for d in range(1, 9):
        pl.when(me >= d)(lambda d=d: halo_copy(d).wait_recv())

    def block(b, window, tokens, chunk, query_rows, key_pos, first_query, first_pos, between):
        unpack[...] = wb[b, :, :, 0:128].reshape(D, 128).astype(F32)
        for g in range(8):
            win[:, 128 * g : 128 * g + 128] = unpack[pl.ds(g, 128, stride=8), :].astype(BF16)
        packed = wa[b, :, :, INNER : 2 * INNER].reshape(64, 16, 512).astype(F32)
        for part in range(2):
            wmix[:, 512 * part : 512 * part + 512] = packed[:, 8 * part : 8 * part + 8].reshape(512, 512).astype(BF16)

        gain = gain_attn[b : b + 1, :]

        def keys(k, _):
            rows = pl.ds(pl.multiple_of(k * chunk, chunk), chunk)
            hidden = jnp.dot(window(k, chunk), win[...], preferred_element_type=F32)
            normed[0:chunk, :] = (hidden * inverse_rms(hidden) * gain).astype(BF16)
            for part in range(2):
                weights = wb[b, :, :, 128 + 512 * part : 640 + 512 * part].reshape(D, 512)
                pairs[rows, 512 * part : 512 * part + 512] = jnp.dot(
                    normed[0:chunk, :], weights, preferred_element_type=F32
                ).astype(BF16)
            return 0

        lax.fori_loop(0, tokens // chunk, keys, 0)
        between(0)
        hidden = jnp.dot(query_rows, win[...], preferred_element_type=F32)
        queries = jnp.dot(
            (hidden * inverse_rms(hidden) * gain).astype(BF16),
            wa[b, :, :, 0:INNER].reshape(D, INNER),
            preferred_element_type=F32,
        ).astype(BF16)
        query_pos = lax.broadcasted_iota(jnp.int32, (ROWS, 1), 0) + first_query
        allowed = (key_pos <= query_pos) & (key_pos > query_pos - WIN) & (key_pos + first_pos >= 0)
        for head in range(HEADS):
            lanes = slice(HS * head, HS * head + HS)
            scores = lax.dot_general(
                queries[:, lanes], pairs[0:tokens, lanes], (((1,), (1,)), ((), ())), preferred_element_type=F32
            )
            scores = jnp.where(allowed, scores, -1e30)
            weights = jnp.exp2((scores - jnp.max(scores, axis=-1, keepdims=True)) * SCALE)
            total = jnp.sum(weights, axis=-1, keepdims=True)
            values = pairs[0:tokens, INNER + HS * head : INNER + HS * head + HS]
            result = jnp.dot(weights.astype(BF16), values, preferred_element_type=F32)
            attended[:, lanes] = (result / total).astype(BF16)
            between(head + 1)
        hidden = hidden + jnp.dot(attended[...], wmix[...], preferred_element_type=F32)
        params[...] = jnp.dot(
            (hidden * inverse_rms(hidden) * gain_head[b : b + 1, :]).astype(BF16),
            wa[b, :, :, 2 * INNER :].reshape(D, 256),
            preferred_element_type=F32,
        )
        shifted = params[EXTRA - 1 : EXTRA - 1 + TOK, :]
        first = (lax.broadcasted_iota(jnp.int32, (TOK, 1), 0) == 0) & (me == 0)
        return jnp.where(first, 0.0, shifted)

    position = lax.broadcasted_iota(jnp.int32, (1, T0), 1)
    shifted = block(
        0,
        lambda k, n: halo[pl.ds(pl.multiple_of(k * n, n), n), :],
        T0,
        384,
        halo[WIN - EXTRA :, :],
        position,
        WIN - EXTRA,
        me * TOK - WIN,
        lambda k: gather.run(steps[1][HOOKS[k] : HOOKS[k + 1]]),
    )
    state[...] = ((latent[...] - shifted[:, :C]) * jnp.exp(-shifted[:, C:])).astype(BF16)

    source = band * 2 + zhi
    high = y % 2

    def first_stage(g):
        return (high * 2 + g // 4) * 4 + g % 4

    def stage_copy(g):
        target = first_stage(g)
        return pltpu.make_async_remote_copy(
            src_ref=state.at[pl.ds(pl.multiple_of(16 * g, 16), 16)],
            dst_ref=tile_a.at[source],
            send_sem=dsend.at[g],
            recv_sem=drecv,
            device_id=(target // 2, (target % 2) * 32 + x * 8 + y),
            device_id_type=MESH,
        )

    def stage_local(g):
        return pltpu.make_async_copy(
            state.at[pl.ds(pl.multiple_of(16 * g, 16), 16)], tile_a.at[source], local_sem
        )

    for g in range(8):
        mine_too = first_stage(g) == source
        pl.when(mine_too)(lambda g=g: stage_local(g).start())
        pl.when(jnp.logical_not(mine_too))(lambda g=g: stage_copy(g).start())

    gather.run(steps[1][HOOKS[5] : HOOKS[6]])
    relay = zlo // 2 == high
    base = 16 * source
    residue = x * 4 + y // 2
    own_offset = x * 4 + y // 2

    def second_copy(o, half, n, at, slot):
        return pltpu.make_async_remote_copy(
            src_ref=tile_b.at[pl.ds(at, n)],
            dst_ref=grid_rows.at[pl.ds(slot, n), residue],
            send_sem=esend.at[2 * o + half],
            recv_sem=erecv,
            device_id=at_device(2 * (base + o) + half),
            device_id_type=MESH,
        )

    def second_local(o, n, at, slot):
        return pltpu.make_async_copy(tile_b.at[pl.ds(at, n)], grid_rows.at[pl.ds(slot, n), residue], erecv)

    def second_each(act, act_local):
        for o in range(20):
            at, slot = max(o - 4, 0), max(4 - o, 0)
            n = min(o, 15) - at + 1
            for half in range(2):
                if o < 16:
                    ours = (own_offset == o) & (y % 2 == half)
                    if act_local is not None:
                        pl.when(ours)(lambda: act_local(second_local(o, n, at, slot)))
                    pl.when(jnp.logical_not(ours))(lambda: act(second_copy(o, half, n, at, slot)))
                else:
                    pl.when(base + o < G)(lambda: act(second_copy(o, half, n, at, slot)))

    @pl.when(relay)
    def _():
        for g in range(8):
            pl.when(first_stage(g) == source)(lambda g=g: stage_local(g).wait())

        pltpu.make_async_remote_copy(
            src_ref=tile_a.at[pl.ds(0, 15)],
            dst_ref=tile_a.at[pl.ds(0, 15)],
            send_sem=dsend.at[0],
            recv_sem=drecv,
            device_id=(band, row),
            device_id_type=MESH,
        ).wait_recv()
        unpack[0:256, :] = tile_a[...].reshape(256, C).astype(F32)
        for c in range(16):
            tile_b[c] = unpack[pl.ds(c, 16, stride=16), :].astype(BF16)
        second_each(lambda copy: copy.start(), lambda copy: copy.start())

    gather.run(steps[1][HOOKS[6] :])

    def slots_got(n):
        pltpu.make_async_remote_copy(
            src_ref=grid_rows.at[pl.ds(5 - n, n)],
            dst_ref=grid_rows.at[pl.ds(5 - n, n)],
            send_sem=esend.at[0],
            recv_sem=erecv,
            device_id=(band, row),
            device_id_type=MESH,
        ).wait_recv()

    for n in range(1, 6):
        pl.when(column + 1 == n if n < 5 else column >= 4)(lambda n=n: slots_got(n))

    unpack[0:256, :] = grid_rows[3].reshape(256, C).astype(F32)
    natural[0:16, :] = unpack[pl.ds(15, 16, stride=16), :]
    unpack[0:256, :] = grid_rows[4].reshape(256, C).astype(F32)
    for m in range(16):
        natural[16 + 16 * m : 32 + 16 * m, :] = unpack[pl.ds(m, 16, stride=16), :]
    query_state[...] = natural[pl.ds(pl.multiple_of(lower * TOK, TOK), ROWS), :]

    place_in = lax.broadcasted_iota(jnp.int32, (1, T1), 1)
    position = place_in // 256 * 256 + place_in % 16 * 16 + place_in // 16 % 16
    shifted = block(
        1,
        lambda k, n: grid_rows[k].reshape(256, C),
        T1,
        256,
        query_state[...].astype(BF16),
        position,
        WIN - EXTRA + lower * TOK,
        (column - 4) * G,
        lambda k: None,
    )
    out[...] = (query_state[EXTRA:, :] - shifted[:, :C]) * jnp.exp(-shifted[:, C:])

    gather.finish()
    for d in range(1, 9):
        pl.when(me + d < DEVICES)(lambda d=d: halo_copy(d).wait_send())
    for g in range(8):
        pl.when(first_stage(g) != source)(lambda g=g: stage_copy(g).wait_send())

    @pl.when(relay)
    def _():
        second_each(lambda copy: copy.wait_send(), None)


def shards(*args):
    vmem = pl.BlockSpec(memory_space=pltpu.VMEM)
    dma = pltpu.SemaphoreType.DMA
    return pl.pallas_call(
        kernel,
        out_shape=jax.ShapeDtypeStruct((TOK, C), F32),
        in_specs=[vmem] * 7,
        out_specs=vmem,
        scratch_shapes=[
            pltpu.VMEM((2, 8, 128, NA), BF16),
            pltpu.VMEM((2, 8, 128, NB), BF16),
            pltpu.VMEM((C, D), BF16),
            pltpu.VMEM((INNER, D), BF16),
            pltpu.VMEM((D, 128), F32),
            pltpu.VMEM((9 * TOK, C), BF16),
            pltpu.VMEM((16, 16, C), BF16),
            pltpu.VMEM((16, 16, C), BF16),
            pltpu.VMEM((5, 16, 16, C), BF16),
            pltpu.VMEM((17 * 16, C), F32),
            pltpu.VMEM((ROWS, C), F32),
            pltpu.VMEM((384, D), BF16),
            pltpu.VMEM((T1, 2 * INNER), BF16),
            pltpu.VMEM((ROWS, INNER), BF16),
            pltpu.VMEM((ROWS, 256), F32),
            pltpu.VMEM((TOK, C), BF16),
            *[dma(shape) for shape in ((2,), (2, 2, 4), (2, 2, 2, 5), (2, 2, 8), (2, 2, 4), (2, 2)) for _ in range(2)],
            dma((9,)),
            dma((9,)),
            dma((8,)),
            dma(()),
            dma((40,)),
            dma(()),
            dma(()),
            pltpu.SemaphoreType.REGULAR,
        ],
        compiler_params=pltpu.CompilerParams(collective_id=0, has_side_effects=True, vmem_limit_bytes=56 << 20),
    )(*args)


def solution(mesh):
    return jax.shard_map(
        shards,
        mesh=mesh,
        in_specs=(
            P(("band", "row"), None),
            P(None, "row", None),
            P(None, "row", None),
            P(None, "row", None),
            P(None, "row", None),
            P(),
            P(),
        ),
        out_specs=P(("band", "row"), None),
        check_vma=False,
    )
```

```python
import math

import jax
import jax.numpy as jnp
from jax import lax
from jax.experimental import pallas as pl
from jax.experimental.pallas import tpu as pltpu
from jax.sharding import PartitionSpec as P

MESH = pl.DeviceIdType.MESH
F32, BF16 = jnp.float32, jnp.bfloat16
G, C, D, HEADS, HS, WIN = 256, 128, 1024, 4, 128, 1024
INNER = HEADS * HS
TOK = 128
DEVICES = 512
NA = INNER + INNER + 256
NB = 128 + 2 * INNER
EXTRA = 16
ROWS = EXTRA + TOK
T0 = WIN + TOK
T1 = 5 * G
EPS = 1e-06
HOOKS = (2, 3, 3, 4, 4, 5, 6)
SCALE = math.log2(math.e) / math.sqrt(HS)


def place():
    band, row = lax.axis_index("band"), lax.axis_index("row")
    return band, row, band // 2, band % 2, row // 32, (row // 8) % 4, row % 8


def at_device(index):
    return (index // 64, index % 64)


class Gather:
    def __init__(self, wa, wb, sems):
        self.wa, self.wb, self.s = wa, wb, sems
        self.band, self.row, self.zlo, self.core, self.zhi, self.x, self.y = place()
        self.z = self.zhi * 4 + self.zlo
        self.sent = ({}, {})

    def at(self, x=None, y=None, zhi=None, core=None):
        x = self.x if x is None else x
        y = self.y if y is None else y
        zhi = self.zhi if zhi is None else zhi
        core = self.core if core is None else core
        return (self.zlo * 2 + core, zhi * 32 + x * 8 + y)

    def copy(self, ref, sem, where):
        name, *index = sem
        if name == "az":
            index[1] = self.half(index[1])
        return pltpu.make_async_remote_copy(
            src_ref=ref,
            dst_ref=ref,
            send_sem=self.s[name][0].at[*index],
            recv_sem=self.s[name][1].at[*index],
            device_id=where,
            device_id_type=MESH,
        )

    def send(self, core, ref, sem, where):
        self.copy(ref, sem, where).start()
        kind = "half" if sem[0] == "side" else "column" if len(ref.shape) == 3 else "cell" if ref.shape[0] == 16 else "line"
        self.sent[core][sem] = kind

    def got(self, ref, sem):
        self.copy(ref, sem, self.at()).wait_recv()

    def half(self, h):
        return self.zhi if h == 0 else 1 - self.zhi

    def cell(self, w, b, h, x, y):
        return w.at[b, 4 * self.half(h) + x, pl.ds(pl.multiple_of(16 * y, 16), 16)]

    def column(self, w, b, h, y, part):
        return w.at[b, pl.ds(4 * self.half(h) + 2 * part, 2), pl.ds(pl.multiple_of(16 * y, 16), 16)]

    def line(self, w, b, h, x):
        return w.at[b, 4 * self.half(h) + x]

    def across(self, core, b):
        w = (self.wa, self.wb)[core]
        self.send(core, self.cell(w, b, 0, self.x, self.y), ("z", b), self.at(zhi=1 - self.zhi))

    def across_got(self, core, b):
        w = (self.wa, self.wb)[core]
        self.got(self.cell(w, b, 1, self.x, self.y), ("z", b))

    def a_x(self, b, h):
        for d in (1, 3, 2):
            self.send(0, self.cell(self.wa, b, h, self.x, self.y), ("ax", b, h, d), self.at(x=(self.x + d) % 4))

    def a_side(self, b, h, y, part):
        self.send(0, self.column(self.wa, b, h, y, part), ("side", b, h), self.at(core=1))

    def a_y(self, b, h, k):
        part = self.z % 2
        if k == 0:
            for d in (1, 3, 2):
                self.got(self.cell(self.wa, b, h, (self.x - d) % 4, self.y), ("ax", b, h, d))
            for d in (2, 6, 1, 7):
                self.a_on(b, h, 0, d)
            self.a_side(b, h, self.y, 0)
            self.a_side(b, h, self.y, 1)
        for d in ((), (2, 6, 1, 7), (3, 5, 4))[k]:
            y = (self.y - d) % 8
            ref = self.column(self.wa, b, h, y, part)
            self.got(ref, ("ay", b, h, d))
            if d == 2:
                self.a_on(b, h, 2, 1)
            if d == 6:
                self.a_on(b, h, 6, 7)
            if d == 2 + 4 * h:
                self.a_on(b, h, d, d)
            z = (self.z + 1 - 2 * self.half(h)) % 8
            self.send(0, ref, ("az", b, h, 8 - d), ((z % 4) * 2 + self.core, (z // 4) * 32 + self.x * 8 + self.y))
            self.a_side(b, h, y, part)

    def a_on(self, b, h, came, d):
        ref = self.column(self.wa, b, h, (self.y - came) % 8, self.z % 2)
        self.send(0, ref, ("ay", b, h, (came + d) % 8), self.at(y=(self.y + d) % 8))

    def a_z(self, b, h, k):
        for d in ((), (2, 6, 1, 7), (3, 5, 4))[k]:
            y = (self.y + d) % 8
            ref = self.column(self.wa, b, h, y, 1 - self.z % 2)
            self.got(ref, ("az", b, h, d))
            self.a_side(b, h, y, 1 - self.z % 2)

    def b_y(self, b, h):
        for d in (4, 3, 5, 2, 6, 1, 7):
            self.send(1, self.cell(self.wb, b, h, self.x, self.y), ("by", b, h, d), self.at(y=(self.y + d) % 8))

    def b_x(self, b, h):
        for d in range(1, 8):
            self.got(self.cell(self.wb, b, h, self.x, (self.y - d) % 8), ("by", b, h, d))
        for d in (1, 3):
            self.send(1, self.line(self.wb, b, h, self.x), ("bx", b, h, d), self.at(x=(self.x + d) % 4))
        self.b_side(b, h, self.x)

    def b_side(self, b, h, x):
        self.send(1, self.line(self.wb, b, h, x), ("side", b, h), self.at(core=0))

    def b_on(self, b, h, d):
        x = (self.x - d) % 4
        self.got(self.line(self.wb, b, h, x), ("bx", b, h, d))
        if d == 1 + 2 * h:
            self.send(1, self.line(self.wb, b, h, x), ("bx", b, h, 2), self.at(x=(self.x + 2 - d) % 4))
        self.b_side(b, h, x)

    def side_got(self, core, b):
        w = (self.wb, self.wa)[core]
        for h in range(2):
            self.got(w.at[b, pl.ds(4 * self.half(h), 4)], ("side", b, h))

    def steps(self, core, b):
        if core == 0:
            yield lambda: self.across(0, b)
            yield lambda: self.a_x(b, 0)
            yield lambda: (self.across_got(0, b), self.a_x(b, 1))
            yield lambda: (self.a_y(b, 0, 0), None)
            yield lambda: (self.a_y(b, 1, 0), None)
            yield lambda: (self.a_y(b, 0, 1), self.a_y(b, 1, 1))
            yield lambda: (self.a_z(b, 0, 1), self.a_z(b, 1, 1))
            yield lambda: (self.a_y(b, 0, 2), self.a_y(b, 1, 2))
            yield lambda: (self.a_z(b, 0, 2), self.a_z(b, 1, 2))
        else:
            yield lambda: self.across(1, b)
            yield lambda: self.b_y(b, 0)
            yield lambda: (self.across_got(1, b), self.b_y(b, 1))
            yield lambda: self.b_x(b, 0)
            yield lambda: self.b_x(b, 1)
            yield lambda: (self.b_on(b, 0, 1), self.b_on(b, 0, 3))
            yield lambda: (self.b_on(b, 1, 3), self.b_on(b, 1, 1), self.b_on(b, 0, 2), self.b_on(b, 1, 2))
            yield lambda: None
            yield lambda: None

    def early(self, b):
        pl.when(self.core == 0)(lambda: self.side_got(0, b))

    def late(self, b):
        pl.when(self.core == 1)(lambda: self.side_got(1, b))

    def run(self, pairs):
        for first, second in pairs:
            pl.when(self.core == 0)(lambda: (first(), None)[1])
            pl.when(self.core == 1)(lambda: (second(), None)[1])

    def finish(self):
        for core in range(2):

            @pl.when(self.core == core)
            def _():
                w = (self.wa, self.wb)[core]
                whole = dict(
                    cell=w.at[0, 0, pl.ds(0, 16)],
                    column=w.at[0, pl.ds(0, 2), pl.ds(0, 16)],
                    line=w.at[0, 0],
                    half=w.at[0, pl.ds(0, 4)],
                )
                for sem, kind in self.sent[core].items():
                    self.copy(whole[kind], sem, self.at()).wait_send()


def inverse_rms(values):
    return lax.rsqrt(jnp.mean(values * values, axis=-1, keepdims=True) + EPS)


def kernel(
    latent, w_in, w_qkv, w_mix, w_head, gain_attn, gain_head, out,
    wa, wb, win, wmix, unpack, halo, tile_a, tile_b, grid_rows, natural, query_state,
    normed, pairs, attended, params, state,
    zsem, zsend, axsem, axsend, aysem, aysend, azsem, azsend, bysem, bysend, bxsem, bxsend, side, side_send,
    hsend, hrecv, dsend, drecv, esend, erecv, local_sem, ready,
):
    band, row, zlo, core, zhi, x, y = place()
    me = band * 64 + row
    before = jnp.minimum(me, 8)

    barrier = pltpu.get_barrier_semaphore()

    def greet(where):
        pl.semaphore_signal(barrier, inc=1, device_id=where, device_id_type=MESH)

    for d in range(1, 8):
        greet((band, row - y + (y + d) % 8))
    for d in range(1, 4):
        greet((band, zhi * 32 + ((x + d) % 4) * 8 + y))
    for d in range(1, 4):
        greet((((zlo + d) % 4) * 2 + core, row))
    greet((band, (row + 32) % 64))
    greet((zlo * 2 + 1 - core, row))
    for d in (1, 7):
        z = (zhi * 4 + zlo + d) % 8
        greet(((z % 4) * 2 + core, (z // 4) * 32 + x * 8 + y))
    tail = row >= 56
    upper, under = tail & (core == 1) & (zlo < 3), tail & (core == 0) & (zlo > 0)
    pl.when(upper)(lambda: greet((band + 1, row)))
    pl.when(under)(lambda: greet((band - 1, row)))

    mine = pl.ds(pl.multiple_of(16 * y, 16), 16)

    @pl.when(core == 0)
    def _():
        for b in range(2):
            wa[b, 4 * zhi + x, mine, 0:INNER] = w_qkv[b, :, 0:INNER]
            mix = w_mix[b].astype(F32)
            wa[b, 4 * zhi + x, mine, INNER : 2 * INNER] = jnp.concatenate(
                [mix[:, :512], mix[:, 512:]], axis=0
            ).astype(BF16)
            wa[b, 4 * zhi + x, mine, 2 * INNER :] = w_head[b]

    @pl.when(core == 1)
    def _():
        for b in range(2):
            wide = w_in[b].astype(F32)
            wb[b, 4 * zhi + x, mine, 0:128] = jnp.concatenate(
                [wide[a : a + 1, 128 * g : 128 * g + 128] for a in range(2) for g in range(8)], axis=0
            ).astype(BF16)
            wb[b, 4 * zhi + x, mine, 128:] = w_qkv[b, :, INNER:]

    halo[8 * TOK :, :] = latent[...].astype(BF16)

    def clear(k, _):
        halo[pl.ds(pl.multiple_of(k * TOK, TOK), TOK), :] = jnp.zeros((TOK, C), BF16)
        return 0

    lax.fori_loop(0, 8 - before, clear, 0)
    column = me // 2
    lower = me % 2

    def clear_column(k, _):
        grid_rows[k] = jnp.zeros((16, 16, C), BF16)
        return 0

    lax.fori_loop(0, jnp.maximum(4 - column, 0), clear_column, 0)

    pl.semaphore_wait(barrier, 17 + (upper | under).astype(jnp.int32))

    sems = dict(
        z=(zsend, zsem),
        ax=(axsend, axsem),
        ay=(aysend, aysem),
        az=(azsend, azsem),
        by=(bysend, bysem),
        bx=(bxsend, bxsem),
        side=(side_send, side),
    )
    gather = Gather(wa, wb, sems)
    steps = [list(zip(gather.steps(0, b), gather.steps(1, b))) for b in range(2)]

    def halo_copy(d):
        return pltpu.make_async_remote_copy(
            src_ref=halo.at[pl.ds(8 * TOK, TOK)],
            dst_ref=halo.at[pl.ds((8 - d) * TOK, TOK)],
            send_sem=hsend.at[d],
            recv_sem=hrecv.at[d],
            device_id=at_device(me + d),
            device_id_type=MESH,
        )

    gather.run(steps[0][:5])
    for d in range(1, 9):
        pl.when(row + d < 64)(lambda d=d: halo_copy(d).start())

    @pl.when(tail & (band > 0))
    def _():
        pl.semaphore_signal(ready, inc=1, device_id=(band - 1, row), device_id_type=MESH)

    gather.run(steps[0][5:6])

    @pl.when(tail & (band < 7))
    def _():
        pl.semaphore_wait(ready, 1)
        for d in range(1, 9):
            pl.when(row + d >= 64)(lambda d=d: halo_copy(d).start())

    gather.run(steps[0][6:7])
    gather.early(0)
    for d in range(1, 9):
        pl.when(me >= d)(lambda d=d: halo_copy(d).wait_recv())

    def block(b, window, tokens, chunk, query_rows, key_pos, first_query, first_pos, between):
        unpack[...] = wb[b, :, :, 0:128].reshape(D, 128).astype(F32)
        for g in range(8):
            win[:, 128 * g : 128 * g + 128] = unpack[pl.ds(g, 128, stride=8), :].astype(BF16)
        gain = gain_attn[b : b + 1, :]

        def keys(k, _):
            rows = pl.ds(pl.multiple_of(k * chunk, chunk), chunk)
            hidden = jnp.dot(window(k, chunk), win[...], preferred_element_type=F32)
            normed[0:chunk, :] = (hidden * inverse_rms(hidden) * gain).astype(BF16)
            for part in range(2):
                weights = wb[b, :, :, 128 + 512 * part : 640 + 512 * part].reshape(D, 512)
                pairs[rows, 512 * part : 512 * part + 512] = jnp.dot(
                    normed[0:chunk, :], weights, preferred_element_type=F32
                ).astype(BF16)
            return 0

        lax.fori_loop(0, tokens // chunk - 1, keys, 0)
        between(-1)
        lax.fori_loop(tokens // chunk - 1, tokens // chunk, keys, 0)
        between(0)
        packed = wa[b, :, :, INNER : 2 * INNER].reshape(64, 16, 512).astype(F32)
        for part in range(2):
            wmix[:, 512 * part : 512 * part + 512] = packed[:, 8 * part : 8 * part + 8].reshape(512, 512).astype(BF16)
        hidden = jnp.dot(query_rows, win[...], preferred_element_type=F32)
        queries = jnp.dot(
            (hidden * inverse_rms(hidden) * gain).astype(BF16),
            wa[b, :, :, 0:INNER].reshape(D, INNER),
            preferred_element_type=F32,
        ).astype(BF16)
        query_pos = lax.broadcasted_iota(jnp.int32, (ROWS, 1), 0) + first_query
        allowed = (key_pos <= query_pos) & (key_pos > query_pos - WIN) & (key_pos + first_pos >= 0)
        for head in range(HEADS):
            lanes = slice(HS * head, HS * head + HS)
            scores = lax.dot_general(
                queries[:, lanes], pairs[0:tokens, lanes], (((1,), (1,)), ((), ())), preferred_element_type=F32
            )
            scores = jnp.where(allowed, scores, -1e30)
            weights = jnp.exp2((scores - jnp.max(scores, axis=-1, keepdims=True)) * SCALE)
            total = jnp.sum(weights, axis=-1, keepdims=True)
            values = pairs[0:tokens, INNER + HS * head : INNER + HS * head + HS]
            result = jnp.dot(weights.astype(BF16), values, preferred_element_type=F32)
            attended[:, lanes] = (result / total).astype(BF16)
            between(head + 1)
        hidden = hidden + jnp.dot(attended[...], wmix[...], preferred_element_type=F32)
        params[...] = jnp.dot(
            (hidden * inverse_rms(hidden) * gain_head[b : b + 1, :]).astype(BF16),
            wa[b, :, :, 2 * INNER :].reshape(D, 256),
            preferred_element_type=F32,
        )
        shifted = params[EXTRA - 1 : EXTRA - 1 + TOK, :]
        first = (lax.broadcasted_iota(jnp.int32, (TOK, 1), 0) == 0) & (me == 0)
        return jnp.where(first, 0.0, shifted)

    def in_block(k):
        if k < 0:
            gather.run(steps[0][7:8])
            gather.run(steps[1][: HOOKS[0]])
            return
        if k == 0:
            gather.run(steps[0][8:])
            gather.late(0)
        gather.run(steps[1][HOOKS[k] : HOOKS[k + 1]])

    position = lax.broadcasted_iota(jnp.int32, (1, T0), 1)
    shifted = block(
        0,
        lambda k, n: halo[pl.ds(pl.multiple_of(k * n, n), n), :],
        T0,
        384,
        halo[WIN - EXTRA :, :],
        position,
        WIN - EXTRA,
        me * TOK - WIN,
        in_block,
    )
    state[...] = ((latent[...] - shifted[:, :C]) * jnp.exp(-shifted[:, C:])).astype(BF16)

    source = band * 2 + zhi
    high = y % 2

    def first_stage(g):
        return (high * 2 + g // 4) * 4 + g % 4

    def stage_copy(g):
        target = first_stage(g)
        return pltpu.make_async_remote_copy(
            src_ref=state.at[pl.ds(pl.multiple_of(16 * g, 16), 16)],
            dst_ref=tile_a.at[source],
            send_sem=dsend.at[g],
            recv_sem=drecv,
            device_id=(target // 2, (target % 2) * 32 + x * 8 + y),
            device_id_type=MESH,
        )

    def stage_local(g):
        return pltpu.make_async_copy(
            state.at[pl.ds(pl.multiple_of(16 * g, 16), 16)], tile_a.at[source], local_sem
        )

    for g in range(8):
        mine_too = first_stage(g) == source
        pl.when(mine_too)(lambda g=g: stage_local(g).start())
        pl.when(jnp.logical_not(mine_too))(lambda g=g: stage_copy(g).start())

    gather.run(steps[1][HOOKS[5] : HOOKS[6]])
    relay = zlo // 2 == high
    base = 16 * source
    residue = x * 4 + y // 2
    own_offset = x * 4 + y // 2

    def second_copy(o, half, n, at, slot):
        return pltpu.make_async_remote_copy(
            src_ref=tile_b.at[pl.ds(at, n)],
            dst_ref=grid_rows.at[pl.ds(slot, n), residue],
            send_sem=esend.at[2 * o + half],
            recv_sem=erecv,
            device_id=at_device(2 * (base + o) + half),
            device_id_type=MESH,
        )

    def second_local(o, n, at, slot):
        return pltpu.make_async_copy(tile_b.at[pl.ds(at, n)], grid_rows.at[pl.ds(slot, n), residue], erecv)

    def second_each(act, act_local):
        for o in range(20):
            at, slot = max(o - 4, 0), max(4 - o, 0)
            n = min(o, 15) - at + 1
            for half in range(2):
                if o < 16:
                    ours = (own_offset == o) & (y % 2 == half)
                    if act_local is not None:
                        pl.when(ours)(lambda: act_local(second_local(o, n, at, slot)))
                    pl.when(jnp.logical_not(ours))(lambda: act(second_copy(o, half, n, at, slot)))
                else:
                    pl.when(base + o < G)(lambda: act(second_copy(o, half, n, at, slot)))

    @pl.when(relay)
    def _():
        for g in range(8):
            pl.when(first_stage(g) == source)(lambda g=g: stage_local(g).wait())

        pltpu.make_async_remote_copy(
            src_ref=tile_a.at[pl.ds(0, 15)],
            dst_ref=tile_a.at[pl.ds(0, 15)],
            send_sem=dsend.at[0],
            recv_sem=drecv,
            device_id=(band, row),
            device_id_type=MESH,
        ).wait_recv()
        unpack[0:256, :] = tile_a[...].reshape(256, C).astype(F32)
        for c in range(16):
            tile_b[c] = unpack[pl.ds(c, 16, stride=16), :].astype(BF16)
        second_each(lambda copy: copy.start(), lambda copy: copy.start())

    gather.run(steps[1][HOOKS[6] :])
    gather.early(1)

    def slots_got(n):
        pltpu.make_async_remote_copy(
            src_ref=grid_rows.at[pl.ds(5 - n, n)],
            dst_ref=grid_rows.at[pl.ds(5 - n, n)],
            send_sem=esend.at[0],
            recv_sem=erecv,
            device_id=(band, row),
            device_id_type=MESH,
        ).wait_recv()

    for n in range(1, 6):
        pl.when(column + 1 == n if n < 5 else column >= 4)(lambda n=n: slots_got(n))

    unpack[0:256, :] = grid_rows[3].reshape(256, C).astype(F32)
    natural[0:16, :] = unpack[pl.ds(15, 16, stride=16), :]
    unpack[0:256, :] = grid_rows[4].reshape(256, C).astype(F32)
    for m in range(16):
        natural[16 + 16 * m : 32 + 16 * m, :] = unpack[pl.ds(m, 16, stride=16), :]
    query_state[...] = natural[pl.ds(pl.multiple_of(lower * TOK, TOK), ROWS), :]

    place_in = lax.broadcasted_iota(jnp.int32, (1, T1), 1)
    position = place_in // 256 * 256 + place_in % 16 * 16 + place_in // 16 % 16
    shifted = block(
        1,
        lambda k, n: grid_rows[k].reshape(256, C),
        T1,
        256,
        query_state[...].astype(BF16),
        position,
        WIN - EXTRA + lower * TOK,
        (column - 4) * G,
        lambda k: gather.late(1) if k == 0 else None,
    )
    out[...] = (query_state[EXTRA:, :] - shifted[:, :C]) * jnp.exp(-shifted[:, C:])

    gather.finish()
    for d in range(1, 9):
        pl.when(me + d < DEVICES)(lambda d=d: halo_copy(d).wait_send())
    for g in range(8):
        pl.when(first_stage(g) != source)(lambda g=g: stage_copy(g).wait_send())

    @pl.when(relay)
    def _():
        second_each(lambda copy: copy.wait_send(), None)


def shards(*args):
    vmem = pl.BlockSpec(memory_space=pltpu.VMEM)
    dma = pltpu.SemaphoreType.DMA
    return pl.pallas_call(
        kernel,
        out_shape=jax.ShapeDtypeStruct((TOK, C), F32),
        in_specs=[vmem] * 7,
        out_specs=vmem,
        scratch_shapes=[
            pltpu.VMEM((2, 8, 128, NA), BF16),
            pltpu.VMEM((2, 8, 128, NB), BF16),
            pltpu.VMEM((C, D), BF16),
            pltpu.VMEM((INNER, D), BF16),
            pltpu.VMEM((D, 128), F32),
            pltpu.VMEM((9 * TOK, C), BF16),
            pltpu.VMEM((16, 16, C), BF16),
            pltpu.VMEM((16, 16, C), BF16),
            pltpu.VMEM((5, 16, 16, C), BF16),
            pltpu.VMEM((17 * 16, C), F32),
            pltpu.VMEM((ROWS, C), F32),
            pltpu.VMEM((384, D), BF16),
            pltpu.VMEM((T1, 2 * INNER), BF16),
            pltpu.VMEM((ROWS, INNER), BF16),
            pltpu.VMEM((ROWS, 256), F32),
            pltpu.VMEM((TOK, C), BF16),
            *[dma(shape) for shape in ((2,), (2, 2, 4), (2, 2, 8), (2, 2, 8), (2, 2, 8), (2, 2, 4), (2, 2)) for _ in range(2)],
            dma((9,)),
            dma((9,)),
            dma((8,)),
            dma(()),
            dma((40,)),
            dma(()),
            dma(()),
            pltpu.SemaphoreType.REGULAR,
        ],
        compiler_params=pltpu.CompilerParams(collective_id=0, has_side_effects=True, vmem_limit_bytes=56 << 20),
    )(*args)


def solution(mesh):
    return jax.shard_map(
        shards,
        mesh=mesh,
        in_specs=(
            P(("band", "row"), None),
            P(None, "row", None),
            P(None, "row", None),
            P(None, "row", None),
            P(None, "row", None),
            P(),
            P(),
        ),
        out_specs=P(("band", "row"), None),
        check_vma=False,
    )
```
